32 devices in a mesh: rows: 8 (over z, x), rep: 4 (over y, core).
Axes of the slice: x: 2, y: 2, z: 4, core: 2. Of those that a mesh axis runs over, the one named last changes fastest.
Arguments:
- p_blocks: bfloat16 [64, 12, 128, 128], P('rows'), may hold values from -1.25 to 1.25
- d_blocks: bfloat16 [64, 12, 128, 128], P('rows'), may hold values from -1.25 to 1.25
- p_cols: int32 [64, 12], replicated, may hold values from 0 to 63, as said below
- d_cols: int32 [64, 12], replicated, may hold values from 0 to 63, as said below
- out_pcols: int32 [64, 12], P('rows'), may hold values from 0 to 63, as said below
- out_dcols: int32 [64, 12], P('rows'), may hold values from 0 to 63, as said below
- row_slot: int32 [64], replicated, may hold values from 0 to 63, as said below
- branch: int32 [64], P('rows'), may hold values from 0 to 1
Outputs:
- next_p: bfloat16 [64, 12, 128, 128], P('rows', 'rep')
- next_d: bfloat16 [64, 12, 128, 128], P('rows', 'rep')
The draws below stay inside these ranges and needn't reach their ends.
Inputs may be any that keep to these rules, and one draw needn't show every extreme that they name: row_slot is a permutation; global block row g is stored at position row_slot[g], on index row_slot[g] // 8 of rows, and never more than 3 positions away from g. `p_cols`: the stored row s that holds global block row g names 12 different global block columns, g among them, each equal to (g + o) mod 64 with -12 <= o <= 12. `d_cols`: as for p_cols. `out_pcols`: as for p_cols. `out_dcols`: as for p_cols.
All inputs are finite; a program needn't handle non-finite values.
Results may differ from the reference program's by a relative error of at most 0.0095.
Values may be sent and summed in bfloat16 or wider, within the bound.
A program may use at most 192 MiB of HBM per device.

```python
import jax
import jax.numpy as jnp
from jax import lax

B = 128
K = 12
KQ = 3
NB = 64
SPREAD = 4


def storage_order(base_key):
    group_count = NB // SPREAD
    scores = jax.random.randint(jax.random.fold_in(base_key, 505), (group_count, SPREAD), 0, 1 << 20) * SPREAD + jnp.arange(SPREAD, dtype=jnp.int32)[None, :]
    local = jnp.argsort(scores, axis=1).astype(jnp.int32)
    order = jnp.arange(group_count, dtype=jnp.int32)[:, None] * SPREAD + local
    return order.reshape(NB).astype(jnp.int32)


def band_columns(base_key, salt_value):
    pattern_key = jax.random.fold_in(base_key, salt_value)
    key_pick, key_slots = jax.random.split(pattern_key)
    offsets = jnp.concatenate([jnp.arange(-K, 0), jnp.arange(1, K + 1)]).astype(jnp.int32)
    scores = jax.random.randint(key_pick, (NB, 2 * K), 0, 1 << 20) * (2 * K) + jnp.arange(2 * K, dtype=jnp.int32)[None, :]
    chosen = jnp.argsort(scores, axis=1)[:, :K - 1]
    global_ids = storage_order(base_key)[:, None]
    columns = jnp.concatenate([global_ids, (global_ids + offsets[chosen]) % NB], axis=1)
    slot_scores = jax.random.randint(key_slots, (NB, K), 0, 1 << 20) * K + jnp.arange(K, dtype=jnp.int32)[None, :]
    slot_order = jnp.argsort(slot_scores, axis=1)
    return jnp.take_along_axis(columns, slot_order, axis=1).astype(jnp.int32)


def draw_p_cols(key, part):
    return band_columns(key, 101)


def draw_d_cols(key, part):
    return band_columns(key, 202)


def draw_out_pcols(key, part):
    return band_columns(key, 303)


def draw_out_dcols(key, part):
    return band_columns(key, 404)


def draw_row_slot(key, part):
    return jnp.argsort(storage_order(key)).astype(jnp.int32)


def plant(result, stream_key, low, top_value):
    shape = result.shape
    place = [jax.random.randint(jax.random.fold_in(stream_key, axis), (), 0, shape[axis]) for axis in range(len(shape))]
    result = result.at[tuple(place)].set(low)
    longest = shape.index(max(shape))
    place[longest] = (place[longest] + 1) % shape[longest]
    return result.at[tuple(place)].set(top_value)


def level_of(rng, extent, cuts, low, high):
    gain, own = 1.0, jax.random.fold_in(rng, 6)
    for axis_at, blocks in cuts:
        draws = jnp.exp(jax.random.uniform(jax.random.fold_in(own, axis_at), (blocks,), jnp.float32, low / len(cuts), high / len(cuts)))
        gain = gain * jnp.repeat(draws, extent[axis_at] // blocks).reshape([-1 if axis == axis_at else 1 for axis in range(len(extent))])
    return gain


def scatter_about(key, dims, spread, limit, cuts=(), kind=jnp.bfloat16):
    values = spread * jax.random.normal(key, dims, jnp.float32)
    if cuts:
        values = values * level_of(key, dims, cuts, -0.22, 0.18)
    return jnp.clip(values, -limit, limit).astype(kind)


def setup_inputs(seed: int = 0) -> dict:
    arg_keys = jax.random.split(jax.random.key(seed), 9)
    p_blocks = scatter_about(arg_keys[0], (NB, K, B, B), 0.2, 1.25, ((0, 8),))
    d_blocks = scatter_about(arg_keys[1], (NB, K, B, B), 0.2, 1.25, ((0, 8),))
    p_cols = draw_p_cols(jax.random.fold_in(arg_keys[8], 71), 0)
    d_cols = draw_d_cols(jax.random.fold_in(arg_keys[8], 71), 0)
    out_pcols = draw_out_pcols(jax.random.fold_in(arg_keys[8], 71), 0)
    out_dcols = draw_out_dcols(jax.random.fold_in(arg_keys[8], 71), 0)
    row_slot = draw_row_slot(jax.random.fold_in(arg_keys[8], 71), 0)
    branch = plant(jax.random.randint(arg_keys[7], (NB,), 0, 2), jax.random.fold_in(arg_keys[7], 1), 0, 1).astype(jnp.int32)
    return dict(p_blocks=p_blocks, d_blocks=d_blocks, p_cols=p_cols, d_cols=d_cols, out_pcols=out_pcols, out_dcols=out_dcols, row_slot=row_slot, branch=branch)


def quarter_products(left_row, left_ids, out_row, right_blocks, right_cols, row_slot):
    stored = jnp.take(row_slot, left_ids, axis=0).astype(jnp.int32)
    right_rows = jnp.take(right_blocks, stored, axis=0).astype(jnp.float32)
    right_ids = jnp.take(right_cols, stored, axis=0)
    block_terms = jnp.einsum("kab,kmbc->kmac", left_row.astype(jnp.float32), right_rows, precision=lax.Precision.HIGHEST)
    matches = (right_ids[:, :, None] == out_row[None, None, :]).astype(jnp.float32)
    matches = matches.reshape(K, K // KQ, KQ, K)
    block_terms = block_terms.reshape(K, K // KQ, KQ, B, B)
    return jnp.einsum("kqmj,kqmac->qjac", matches, block_terms, precision=lax.Precision.HIGHEST)


def rounded_sum(quarter_parts):
    narrow = lax.optimization_barrier(quarter_parts.astype(jnp.bfloat16))
    return jnp.sum(narrow.astype(jnp.float32), axis=0)


def kept_blocks(row_blocks, row_ids, out_row):
    matches = (row_ids[:, None] == out_row[None, :]).astype(jnp.float32)
    return jnp.einsum("kj,kab->jab", matches, row_blocks.astype(jnp.float32), precision=lax.Precision.HIGHEST)


def reference(p_blocks, d_blocks, p_cols, d_cols, out_pcols, out_dcols, row_slot, branch):
    def one_row(row_items):
        p_row, d_row, p_ids, d_ids, p_out, d_out, row_bit = row_items
        squaring = row_bit == 1
        square = rounded_sum(quarter_products(p_row, p_ids, p_out, p_blocks, p_cols, row_slot))
        tangent = rounded_sum(quarter_products(p_row, p_ids, d_out, d_blocks, d_cols, row_slot) + quarter_products(d_row, d_ids, d_out, p_blocks, p_cols, row_slot))
        p_kept = kept_blocks(p_row, p_ids, p_out)
        d_kept = kept_blocks(d_row, d_ids, d_out)
        new_p = jnp.where(squaring, square, 2.0 * p_kept - square).astype(jnp.bfloat16)
        new_d = jnp.where(squaring, tangent, 2.0 * d_kept - tangent).astype(jnp.bfloat16)
        return new_p, new_d

    next_p, next_d = lax.map(one_row, (p_blocks, d_blocks, p_cols, d_cols, out_pcols, out_dcols, branch))
    return next_p, next_d
```

```python
import functools

import jax
import jax.numpy as jnp
from jax import lax
from jax.experimental import pallas as pl
from jax.experimental.pallas import tpu as pltpu
from jax.sharding import PartitionSpec as P

MESH = pl.DeviceIdType.MESH
MOVE = 3


def nt_dot(left, right):
    return lax.dot_general(
        left, right, (((1,), (1,)), ((), ())), preferred_element_type=jnp.float32
    )


def pack_kernel(pick_ref, p_ref, d_ref, out_ref):
    slots, side = p_ref.shape[1], p_ref.shape[2]
    width = pick_ref.shape[0]
    for which, ref in enumerate((p_ref, d_ref)):
        cut = nt_dot(pick_ref[...], ref[0].reshape(slots * side, side)).astype(jnp.bfloat16)
        for m in range(slots):
            out_ref[0, which, m * width : (m + 1) * width, :] = cut[:, m * side : (m + 1) * side]


def pack(pick, p_blocks, d_blocks):
    rows, slots, side, _ = p_blocks.shape
    width = pick.shape[0]
    block = pl.BlockSpec((1, slots, side, side), lambda s: (s, 0, 0, 0))
    return pl.pallas_call(
        pack_kernel,
        grid=(rows,),
        in_specs=[pl.BlockSpec((width, side), lambda s: (0, 0)), block, block],
        out_specs=pl.BlockSpec((1, 2, slots * width, side), lambda s: (s, 0, 0, 0)),
        out_shape=jax.ShapeDtypeStruct((rows, 2, slots * width, side), jnp.bfloat16),
    )(pick, p_blocks, d_blocks)


def gather_kernel(count, chunks, base, own_ref, cand_ref, send_sem, recv_sem, local_sem):
    me = lax.axis_index("rows")
    parity = lax.rem(me, 2)
    sign = 1 - 2 * parity

    def at(distance):
        return lax.rem(me + distance + 4 * count, count)

    partner, far, back, edge_dev = at(sign), at(2 * sign), at(-2 * sign), at(-3 * sign)
    barrier = pltpu.get_barrier_semaphore()
    for other in (partner, far, back, edge_dev):
        pl.semaphore_signal(barrier, inc=1, device_id={"rows": other}, device_id_type=MESH)
    pl.semaphore_wait(barrier, 4)

    def copy(src, place, sem, device):
        return pltpu.make_async_remote_copy(
            src_ref=src,
            dst_ref=cand_ref.at[place],
            send_sem=send_sem.at[sem],
            recv_sem=recv_sem.at[sem],
            device_id={"rows": device},
            device_id_type=MESH,
        )

    def slot(distance, chunk):
        return base + distance * chunks + chunk

    to_back = [copy(own_ref.at[c], slot(2 * sign, c), c, back) for c in range(chunks)]
    to_partner = [copy(own_ref.at[c], slot(-sign, c), chunks + c, partner) for c in range(chunks)]
    to_far = [copy(own_ref.at[c], slot(-2 * sign, c), 2 * chunks + c, far) for c in range(chunks)]
    first = parity * (chunks - 1)
    last = (1 - parity) * (chunks - 1)
    edge = copy(own_ref.at[first], slot(3 * sign, first), 4 * chunks, edge_dev)
    stay = pltpu.make_async_copy(own_ref, cand_ref.at[pl.ds(base, chunks)], local_sem)
    for c in range(chunks):
        to_back[c].start()
        to_far[c].start()
        to_partner[c].start()
    edge.start()
    stay.start()

    def arrived(distance, chunk, sem):
        place = slot(distance, chunk)
        copy(cand_ref.at[place], place, sem, partner).wait_recv()

    onward = []
    for c in range(chunks):
        arrived(2 * sign, c, c)
        passed = copy(cand_ref.at[slot(2 * sign, c)], slot(sign, c), 3 * chunks + c, partner)
        passed.start()
        onward.append(passed)
    arrived(-2 * sign, last, 2 * chunks + last)
    passed = copy(
        cand_ref.at[slot(-2 * sign, last)], slot(-3 * sign, last), 4 * chunks + 1, partner
    )
    passed.start()
    onward.append(passed)

    for c in range(chunks):
        arrived(sign, c, chunks + c)
    for i in range(1, chunks):
        rest = lax.rem(last + i, chunks)
        arrived(-2 * sign, rest, 2 * chunks + rest)
    for c in range(chunks):
        arrived(-sign, c, 3 * chunks + c)
    arrived(-3 * sign, last, 4 * chunks)
    arrived(3 * sign, first, 4 * chunks + 1)
    for sent in (*to_back, *to_partner, *to_far, edge, *onward):
        sent.wait_send()
    stay.wait()


def gather(packed, count, margin):
    rows = packed.shape[0]
    chunk = margin - 2 * rows
    chunks, base = rows // chunk, margin // chunk
    tail = packed.shape[1:]
    places = 2 * base + chunks
    out = pl.pallas_call(
        functools.partial(gather_kernel, count, chunks, base),
        in_specs=[pl.BlockSpec(memory_space=pl.ANY)],
        out_specs=pl.BlockSpec(memory_space=pl.ANY),
        out_shape=jax.ShapeDtypeStruct((places, chunk, *tail), packed.dtype),
        scratch_shapes=[
            pltpu.SemaphoreType.DMA((4 * chunks + 2,)),
            pltpu.SemaphoreType.DMA((4 * chunks + 2,)),
            pltpu.SemaphoreType.DMA,
        ],
        compiler_params=pltpu.CompilerParams(collective_id=0, has_side_effects=True),
    )(packed.reshape(chunks, chunk, *tail))
    return out.reshape(places * chunk, *tail)


def multiply_kernel(table_ref, p_ref, d_ref, cand_ref, out_ref, right, left):
    slots, side = p_ref.shape[1], p_ref.shape[2]
    reps, _, _, quarter, width, _ = out_ref.shape
    s = pl.program_id(0)
    sums = []
    for pairs in ((0,), (1, 2)):
        total = None
        for pair in pairs:
            lref = d_ref if pair == 2 else p_ref
            for k in range(slots):
                left[:, k * side : (k + 1) * side] = lref[0, k]
                for j in range(slots):
                    place = table_ref[pair, s, k, j]
                    right[pair, j * width : (j + 1) * width, k * side : (k + 1) * side] = cand_ref[
                        place
                    ]
            part = nt_dot(right[pair], left[...])
            total = part if total is None else total + part
        sums.append(total)
    for which, total in enumerate(sums):
        out_ref[:, 0, which] = total.astype(jnp.bfloat16).reshape(reps, quarter, width, side)


def multiply(table, p_blocks, d_blocks, cand, reps):
    rows, slots, side, _ = p_blocks.shape
    width = cand.shape[1]
    quarter = slots // reps
    block = pl.BlockSpec((1, slots, side, side), lambda s, t: (s, 0, 0, 0))
    return pl.pallas_call(
        multiply_kernel,
        grid_spec=pltpu.PrefetchScalarGridSpec(
            num_scalar_prefetch=1,
            grid=(rows,),
            in_specs=[block, block, pl.BlockSpec(memory_space=pltpu.VMEM)],
            out_specs=pl.BlockSpec(
                (reps, 1, 2, quarter, width, side), lambda s, t: (0, s, 0, 0, 0, 0)
            ),
            scratch_shapes=[
                pltpu.VMEM((3, slots * width, slots * side), jnp.bfloat16),
                pltpu.VMEM((side, slots * side), jnp.bfloat16),
            ],
        ),
        out_shape=jax.ShapeDtypeStruct((reps, rows, 2, quarter, width, side), jnp.bfloat16),
        compiler_params=pltpu.CompilerParams(vmem_limit_bytes=48 * 1024 * 1024),
    )(table, p_blocks, d_blocks, cand)


def finish_kernel(keep_ref, bit_ref, eye_ref, sum_ref, p_ref, d_ref, outp_ref, outd_ref):
    quarter, side = outp_ref.shape[1], outp_ref.shape[2]
    slots = p_ref.shape[1]
    s = pl.program_id(0)
    squaring = bit_ref[s] == 1
    for which, (ref, out) in enumerate(((p_ref, outp_ref), (d_ref, outd_ref))):
        for j in range(quarter):
            total = nt_dot(eye_ref[...], sum_ref[:, 0, which, j].reshape(side, side))
            place = keep_ref[which, s, j]
            kept = ref[0, jnp.minimum(place, slots - 1)].astype(jnp.float32)
            kept = jnp.where(place < slots, kept, 0.0)
            out[0, j] = jnp.where(squaring, total, 2.0 * kept - total).astype(jnp.bfloat16)


def finish(keep, bits, eye, sums, p_blocks, d_blocks):
    rows, slots, side, _ = p_blocks.shape
    reps, _, _, quarter, width, _ = sums.shape
    block = pl.BlockSpec((1, slots, side, side), lambda s, k, b: (s, 0, 0, 0))
    out = pl.BlockSpec((1, quarter, side, side), lambda s, k, b: (s, 0, 0, 0))
    shape = jax.ShapeDtypeStruct((rows, quarter, side, side), jnp.bfloat16)
    return pl.pallas_call(
        finish_kernel,
        grid_spec=pltpu.PrefetchScalarGridSpec(
            num_scalar_prefetch=2,
            grid=(rows,),
            in_specs=[
                pl.BlockSpec((side, side), lambda s, k, b: (0, 0)),
                pl.BlockSpec((reps, 1, 2, quarter, width, side), lambda s, k, b: (0, s, 0, 0, 0, 0)),
                block,
                block,
            ],
            out_specs=[out, out],
        ),
        out_shape=[shape, shape],
    )(keep, bits, eye, sums, p_blocks, d_blocks)


def local(p_blocks, d_blocks, p_cols, d_cols, out_pcols, out_dcols, row_slot, branch):
    rows, slots, side = p_blocks.shape[:3]
    reps, count = lax.axis_size("rep"), lax.axis_size("rows")
    quarter, width = slots // reps, side // reps
    all_rows = rows * count
    margin = slots + 2 * MOVE
    row_start = lax.axis_index("rows") * rows
    rep = lax.axis_index("rep")

    pick = (
        jnp.arange(width, dtype=jnp.int32)[:, None] + rep * width
        == jnp.arange(side, dtype=jnp.int32)[None, :]
    ).astype(jnp.bfloat16)
    packed = pack(pick, p_blocks, d_blocks)
    cand = gather(packed, count, margin)
    cand_rows = cand.shape[0]
    blocks = cand.reshape(cand_rows * 2 * slots, width, side)
    nothing = cand_rows * 2 * slots
    blocks = jnp.concatenate([blocks, jnp.zeros((1, width, side), blocks.dtype)], axis=0)

    own_p = lax.dynamic_slice_in_dim(p_cols, row_start, rows, 0)
    own_d = lax.dynamic_slice_in_dim(d_cols, row_start, rows, 0)
    every = jnp.arange(all_rows, dtype=jnp.int32)
    slot_range = jnp.arange(slots, dtype=jnp.int32)

    def locate(ids):
        stored = jnp.sum(jnp.where(ids[:, :, None] == every, row_slot, 0), axis=2)
        return stored, (stored - row_start + margin) % all_rows

    stored_p, near_p = locate(own_p)
    stored_d, near_d = locate(own_d)

    def entries(stored, near, right_cols, which, out_ids):
        right = jnp.sum(
            jnp.where((stored[:, :, None] == every)[..., None], right_cols, 0), axis=2
        )
        matches = right[:, :, :, None] == out_ids[:, None, None, :]
        m = jnp.sum(jnp.where(matches, slot_range[:, None] + 1, 0), axis=2)
        return jnp.where(m > 0, (near[:, :, None] * 2 + which) * slots + m - 1, nothing)

    table = jnp.stack(
        [
            entries(stored_p, near_p, p_cols, 0, out_pcols),
            entries(stored_p, near_p, d_cols, 1, out_dcols),
            entries(stored_d, near_d, p_cols, 0, out_dcols),
        ]
    ).astype(jnp.int32)

    def positions(ids, out_ids):
        out_ids = lax.dynamic_slice_in_dim(out_ids, rep * quarter, quarter, 1)
        matches = ids[:, :, None] == out_ids[:, None, :]
        found = jnp.sum(jnp.where(matches, slot_range[:, None] + 1, 0), axis=1)
        return jnp.where(found > 0, found - 1, slots)

    keep = jnp.stack([positions(own_p, out_pcols), positions(own_d, out_dcols)]).astype(jnp.int32)
    parts = multiply(table, p_blocks, d_blocks, blocks, reps)
    sums = lax.all_to_all(parts, "rep", 0, 0)
    eye = jnp.eye(side, dtype=jnp.bfloat16)
    next_p, next_d = finish(keep, branch, eye, sums, p_blocks, d_blocks)
    return next_p, next_d


def solution(mesh):
    return jax.shard_map(
        local,
        mesh=mesh,
        in_specs=(
            P("rows", None, None, None),
            P("rows", None, None, None),
            P(),
            P(),
            P("rows", None),
            P("rows", None),
            P(),
            P("rows"),
        ),
        out_specs=(P("rows", "rep", None, None), P("rows", "rep", None, None)),
        check_vma=False,
    )
```

```python
import functools

import jax
import jax.numpy as jnp
from jax import lax
from jax.experimental import pallas as pl
from jax.experimental.pallas import tpu as pltpu
from jax.sharding import PartitionSpec as P

MESH = pl.DeviceIdType.MESH
MOVE = 3


def nt_dot(left, right):
    return lax.dot_general(
        left, right, (((1,), (1,)), ((), ())), preferred_element_type=jnp.float32
    )


def step_kernel(
    margin, table_ref, bit_ref, pick_ref, eye_ref, p_ref, d_ref, outp_ref, outd_ref,
    cand, right, left, parts, sums, send_sem, recv_sem, give_sem, take_sem,
):
    count, reps = lax.axis_size("rows"), lax.axis_size("rep")
    rows, slots, side = p_ref.shape[0], p_ref.shape[1], p_ref.shape[2]
    width, quarter = side // reps, slots // reps
    chunk = margin - 2 * rows
    chunks, base = rows // chunk, margin // chunk
    length = chunk * 2 * slots
    me, rep = lax.axis_index("rows"), lax.axis_index("rep")
    parity = lax.rem(me, 2)
    sign = 1 - 2 * parity

    def at(distance):
        return lax.rem(me + distance + 4 * count, count)

    partner, far, back, edge_dev = at(sign), at(2 * sign), at(-2 * sign), at(-3 * sign)
    barrier = pltpu.get_barrier_semaphore()
    for other in (partner, far, back, edge_dev):
        pl.semaphore_signal(barrier, inc=1, device_id={"rows": other}, device_id_type=MESH)
    for hop in range(1, reps):
        pl.semaphore_signal(
            barrier, inc=1, device_id={"rep": lax.rem(rep + hop, reps)}, device_id_type=MESH
        )

    def pack(c):
        for row in range(c * chunk, (c + 1) * chunk):
            for which, ref in enumerate((p_ref, d_ref)):
                cut = nt_dot(pick_ref[...], ref[row].reshape(slots * side, side))
                cut = cut.astype(jnp.bfloat16)
                for m in range(slots):
                    cand[((margin + row) * 2 + which) * slots + m] = cut[
                        :, m * side : (m + 1) * side
                    ]

    pack(0)
    cand[cand.shape[0] - 1] = jnp.zeros((width, side), jnp.bfloat16)
    pl.semaphore_wait(barrier, 3 + reps)

    def slot(distance, piece):
        return base + distance * chunks + piece

    def copy(source, place, sem, device):
        return pltpu.make_async_remote_copy(
            src_ref=cand.at[pl.ds(source * length, length)],
            dst_ref=cand.at[pl.ds(place * length, length)],
            send_sem=send_sem.at[sem],
            recv_sem=recv_sem.at[sem],
            device_id={"rows": device},
            device_id_type=MESH,
        )

    first = parity * (chunks - 1)
    last = (1 - parity) * (chunks - 1)
    sent = []

    def send(*where):
        sent.append(copy(*where))
        sent[-1].start()

    for c in range(chunks):
        if c:
            pack(c)
        send(base + c, slot(2 * sign, c), c, back)
        send(base + c, slot(-2 * sign, c), 2 * chunks + c, far)
        send(base + c, slot(-sign, c), chunks + c, partner)
    send(base + first, slot(3 * sign, first), 4 * chunks, edge_dev)

    def arrived(distance, piece, sem):
        place = slot(distance, piece)
        copy(place, place, sem, partner).wait_recv()

    for c in range(chunks):
        arrived(2 * sign, c, c)
        send(slot(2 * sign, c), slot(sign, c), 3 * chunks + c, partner)
    arrived(-2 * sign, last, 2 * chunks + last)
    send(slot(-2 * sign, last), slot(-3 * sign, last), 4 * chunks + 1, partner)
    for c in range(chunks):
        arrived(sign, c, chunks + c)
    for i in range(1, chunks):
        rest = lax.rem(last + i, chunks)
        arrived(-2 * sign, rest, 2 * chunks + rest)
    for c in range(chunks):
        arrived(-sign, c, 3 * chunks + c)
    arrived(-3 * sign, last, 4 * chunks)
    arrived(3 * sign, first, 4 * chunks + 1)
    for started in sent:
        started.wait_send()

    def exchange(s, hop):
        to = lax.rem(rep + hop, reps)
        return pltpu.make_async_remote_copy(
            src_ref=parts.at[s, to],
            dst_ref=sums.at[rep, s],
            send_sem=give_sem.at[s, hop - 1],
            recv_sem=take_sem.at[s, hop - 1],
            device_id={"rep": to},
            device_id_type=MESH,
        )

    span = slots * side

    def one_row(s, carry):
        for k in range(slots):
            left[:, k * side : (k + 1) * side] = p_ref[s, k]
            left[:, span + k * side : span + (k + 1) * side] = d_ref[s, k]
        for pair in range(3):
            for k in range(slots):
                for j in range(slots):
                    place = table_ref[((pair * rows + s) * slots + k) * slots + j]
                    right[
                        j * width : (j + 1) * width,
                        pair * span + k * side : pair * span + (k + 1) * side,
                    ] = cand[place]
        squaring = bit_ref[s] == 1
        square = nt_dot(right[:, :span], left[:, :span])
        tangent = nt_dot(right[:, span:], left[...])
        for which, total in enumerate((square, tangent)):
            for j in range(slots):
                kept = cand[table_ref[(3 * slots + which) * rows * slots + s * slots + j]]
                part = total[j * width : (j + 1) * width]
                new = jnp.where(squaring, part, 2.0 * kept.astype(jnp.float32) - part)
                start = (which * quarter + j % quarter) * width
                parts[s, j // quarter, start : start + width] = new.astype(jnp.bfloat16)
        for hop in range(1, reps):
            exchange(s, hop).start()
        return carry

    lax.fori_loop(0, rows, one_row, 0)

    def finish_row(s, carry):
        for hop in range(1, reps):
            came = lax.rem(rep + reps - hop, reps)
            pltpu.make_async_remote_copy(
                src_ref=sums.at[came, s],
                dst_ref=sums.at[came, s],
                send_sem=give_sem.at[s, hop - 1],
                recv_sem=take_sem.at[s, hop - 1],
                device_id={"rep": came},
                device_id_type=MESH,
            ).wait_recv()
        sums[rep, s] = parts[s, rep]
        for which, out in enumerate((outp_ref, outd_ref)):
            for j in range(quarter):
                start = (which * quarter + j) * width
                turned = sums[:, s, start : start + width, :].reshape(side, side)
                out[s, j] = nt_dot(eye_ref[...], turned).astype(jnp.bfloat16)
        for hop in range(1, reps):
            exchange(s, hop).wait_send()
        return carry

    lax.fori_loop(0, rows, finish_row, 0)


def step(margin, reps, table, bits, pick, eye, p_blocks, d_blocks):
    rows, slots, side, _ = p_blocks.shape
    width, quarter = side // reps, slots // reps
    chunks = rows // (margin - 2 * rows)
    shape = jax.ShapeDtypeStruct((rows, quarter, side, side), jnp.bfloat16)
    vmem = pl.BlockSpec(memory_space=pltpu.VMEM)
    smem = pl.BlockSpec(memory_space=pltpu.SMEM)
    return pl.pallas_call(
        functools.partial(step_kernel, margin),
        in_specs=[smem, smem, vmem, vmem, vmem, vmem],
        out_specs=[vmem, vmem],
        out_shape=[shape, shape],
        scratch_shapes=[
            pltpu.VMEM(((rows + 2 * margin) * 2 * slots + 1, width, side), jnp.bfloat16),
            pltpu.VMEM((slots * width, 3 * slots * side), jnp.bfloat16),
            pltpu.VMEM((side, 2 * slots * side), jnp.bfloat16),
            pltpu.VMEM((rows, reps, 2 * quarter * width, side), jnp.bfloat16),
            pltpu.VMEM((reps, rows, 2 * quarter * width, side), jnp.bfloat16),
            pltpu.SemaphoreType.DMA((4 * chunks + 2,)),
            pltpu.SemaphoreType.DMA((4 * chunks + 2,)),
            pltpu.SemaphoreType.DMA((rows, reps - 1)),
            pltpu.SemaphoreType.DMA((rows, reps - 1)),
        ],
        compiler_params=pltpu.CompilerParams(
            collective_id=0, has_side_effects=True, vmem_limit_bytes=48 * 1024 * 1024
        ),
    )(table, bits, pick, eye, p_blocks, d_blocks)


def local(p_blocks, d_blocks, p_cols, d_cols, out_pcols, out_dcols, row_slot, branch):
    rows, slots, side = p_blocks.shape[:3]
    reps, count = lax.axis_size("rep"), lax.axis_size("rows")
    width = side // reps
    all_rows = rows * count
    margin = slots + 2 * MOVE
    row_start = lax.axis_index("rows") * rows
    rep = lax.axis_index("rep")

    pick = (
        jnp.arange(width, dtype=jnp.int32)[:, None] + rep * width
        == jnp.arange(side, dtype=jnp.int32)[None, :]
    ).astype(jnp.bfloat16)
    eye = jnp.eye(side, dtype=jnp.bfloat16)
    nothing = (rows + 2 * margin) * 2 * slots

    own_p = lax.dynamic_slice_in_dim(p_cols, row_start, rows, 0)
    own_d = lax.dynamic_slice_in_dim(d_cols, row_start, rows, 0)
    every = jnp.arange(all_rows, dtype=jnp.int32)
    slot_range = jnp.arange(slots, dtype=jnp.int32)
    ids = jnp.concatenate([own_p, own_d]).reshape(-1)
    stored = jnp.sum(jnp.where(ids[:, None] == every, row_slot, 0), axis=1)
    near = ((stored - row_start + margin) % all_rows).reshape(2, rows, slots)
    one_hot = (stored[:, None] == every).astype(jnp.float32)
    columns = jnp.concatenate([p_cols, d_cols], axis=1).astype(jnp.float32)
    named = jnp.dot(one_hot, columns, precision=lax.Precision.HIGHEST)
    named = jnp.round(named).astype(jnp.int32).reshape(2, rows, slots, 2, slots)

    def entries(left, which, out_ids):
        matches = named[left, :, :, which, :, None] == out_ids[:, None, None, :]
        m = jnp.sum(jnp.where(matches, slot_range[:, None] + 1, 0), axis=2)
        return jnp.where(m > 0, (near[left, :, :, None] * 2 + which) * slots + m - 1, nothing)

    def positions(ids, which, out_ids):
        matches = ids[:, :, None] == out_ids[:, None, :]
        found = jnp.sum(jnp.where(matches, slot_range[:, None] + 1, 0), axis=1)
        own = margin + jnp.arange(rows, dtype=jnp.int32)[:, None]
        return jnp.where(found > 0, (own * 2 + which) * slots + found - 1, nothing)

    table = jnp.concatenate(
        [
            entries(0, 0, out_pcols).reshape(-1),
            entries(0, 1, out_dcols).reshape(-1),
            entries(1, 0, out_dcols).reshape(-1),
            positions(own_p, 0, out_pcols).reshape(-1),
            positions(own_d, 1, out_dcols).reshape(-1),
        ]
    ).astype(jnp.int32)
    next_p, next_d = step(margin, reps, table, branch, pick, eye, p_blocks, d_blocks)
    return next_p, next_d


def solution(mesh):
    return jax.shard_map(
        local,
        mesh=mesh,
        in_specs=(
            P("rows", None, None, None),
            P("rows", None, None, None),
            P(),
            P(),
            P("rows", None),
            P("rows", None),
            P(),
            P("rows"),
        ),
        out_specs=(P("rows", "rep", None, None), P("rows", "rep", None, None)),
        check_vma=False,
    )
```

```python
import functools

import jax
import jax.numpy as jnp
from jax import lax
from jax.experimental import pallas as pl
from jax.experimental.pallas import tpu as pltpu
from jax.sharding import PartitionSpec as P

MESH = pl.DeviceIdType.MESH
MOVE = 3


def nt_dot(left, right):
    return lax.dot_general(
        left, right, (((1,), (1,)), ((), ())), preferred_element_type=jnp.float32
    )


def step_kernel(
    margin, table_ref, bit_ref, pick_ref, eye_ref, p_ref, d_ref, outp_ref, outd_ref,
    near_p, near_d, right, left, later, parts, sums, send_sem, recv_sem, give_sem, take_sem,
):
    count, reps = lax.axis_size("rows"), lax.axis_size("rep")
    rows, slots, side = p_ref.shape[0], p_ref.shape[1], p_ref.shape[2]
    width, quarter = side // reps, slots // reps
    chunk = margin - 2 * rows
    chunks, base = rows // chunk, margin // chunk
    length = chunk * slots
    me, rep = lax.axis_index("rows"), lax.axis_index("rep")
    parity = lax.rem(me, 2)
    sign = 1 - 2 * parity
    near = (near_p, near_d)

    def at(distance):
        return lax.rem(me + distance + 4 * count, count)

    partner, far, back, edge_dev = at(sign), at(2 * sign), at(-2 * sign), at(-3 * sign)
    barrier = pltpu.get_barrier_semaphore()
    for other in (partner, far, back, edge_dev):
        pl.semaphore_signal(barrier, inc=1, device_id={"rows": other}, device_id_type=MESH)
    for hop in range(1, reps):
        pl.semaphore_signal(
            barrier, inc=1, device_id={"rep": lax.rem(rep + hop, reps)}, device_id_type=MESH
        )

    def pack(which, c):
        ref = (p_ref, d_ref)[which]
        for row in range(c * chunk, (c + 1) * chunk):
            cut = nt_dot(pick_ref[...], ref[row].reshape(slots * side, side))
            cut = cut.astype(jnp.bfloat16)
            for m in range(slots):
                near[which][(margin + row) * slots + m] = cut[:, m * side : (m + 1) * side]

    pack(0, 0)
    pl.semaphore_wait(barrier, 3 + reps)

    def slot(distance, piece):
        return base + distance * chunks + piece

    def copy(which, source, place, sem, device):
        return pltpu.make_async_remote_copy(
            src_ref=near[which].at[pl.ds(source * length, length)],
            dst_ref=near[which].at[pl.ds(place * length, length)],
            send_sem=send_sem.at[which, sem],
            recv_sem=recv_sem.at[which, sem],
            device_id={"rows": device},
            device_id_type=MESH,
        )

    first = parity * (chunks - 1)
    last = (1 - parity) * (chunks - 1)
    sent = ([], [])

    def send(which, *where):
        sent[which].append(copy(which, *where))
        sent[which][-1].start()

    def to_partner(which, c):
        send(which, base + c, slot(-sign, c), chunks + c, partner)

    def to_others(which, c):
        send(which, base + c, slot(2 * sign, c), c, back)
        send(which, base + c, slot(-2 * sign, c), 2 * chunks + c, far)

    def to_edge(which):
        send(which, base + first, slot(3 * sign, first), 4 * chunks, edge_dev)

    def arrived(which, distance, piece, sem):
        place = slot(distance, piece)
        copy(which, place, place, sem, partner).wait_recv()

    def forward(which, c):
        arrived(which, 2 * sign, c, c)
        send(which, slot(2 * sign, c), slot(sign, c), 3 * chunks + c, partner)

    def forward_edge(which):
        arrived(which, -2 * sign, last, 2 * chunks + last)
        send(which, slot(-2 * sign, last), slot(-3 * sign, last), 4 * chunks + 1, partner)

    def settle(which):
        for c in range(chunks):
            arrived(which, sign, c, chunks + c)
        for i in range(1, chunks):
            rest = lax.rem(last + i, chunks)
            arrived(which, -2 * sign, rest, 2 * chunks + rest)
        for c in range(chunks):
            arrived(which, -sign, c, 3 * chunks + c)
        arrived(which, -3 * sign, last, 4 * chunks)
        arrived(which, 3 * sign, first, 4 * chunks + 1)

    for c in range(chunks):
        if c:
            pack(0, c)
        to_others(0, c)
        to_partner(0, c)
    to_edge(0)
    for c in range(chunks):
        pack(1, c)
        to_others(1, c)
    to_edge(1)
    for ref in near:
        ref[ref.shape[0] - 1] = jnp.zeros((width, side), jnp.bfloat16)
    for c in range(chunks):
        forward(0, c)
    forward_edge(0)
    for c in range(chunks):
        to_partner(1, c)
    settle(0)

    def exchange(which, s, hop):
        to = lax.rem(rep + hop, reps)
        return pltpu.make_async_remote_copy(
            src_ref=parts.at[which, s, to],
            dst_ref=sums.at[which, rep, s],
            send_sem=give_sem.at[which, s, hop - 1],
            recv_sem=take_sem.at[which, s, hop - 1],
            device_id={"rep": to},
            device_id_type=MESH,
        )

    span = slots * side

    def collect(pair, s, source):
        for k in range(slots):
            for j in range(slots):
                place = table_ref[((pair * rows + s) * slots + k) * slots + j]
                right[pair, j * width : (j + 1) * width, k * side : (k + 1) * side] = source[place]

    def line_up(s, spot, ref):
        for k in range(slots):
            left[spot, :, k * side : (k + 1) * side] = ref[s, k]

    def conclude(which, s, total):
        squaring = bit_ref[s] == 1
        for j in range(slots):
            kept = near[which][table_ref[(3 * slots + which) * rows * slots + s * slots + j]]
            part = total[j * width : (j + 1) * width]
            new = jnp.where(squaring, part, 2.0 * kept.astype(jnp.float32) - part)
            start = (j % quarter) * width
            parts[which, s, j // quarter, start : start + width] = new.astype(jnp.bfloat16)
        for hop in range(1, reps):
            exchange(which, s, hop).start()

    def early_row(s, carry):
        line_up(s, 0, p_ref)
        line_up(s, 1, d_ref)
        collect(0, s, near_p)
        collect(2, s, near_p)
        square = nt_dot(right[0], left[0])
        later[s] = nt_dot(right[2], left[1])
        conclude(0, s, square)
        return carry

    def late_row(s, carry):
        line_up(s, 0, p_ref)
        collect(1, s, near_d)
        conclude(1, s, later[s] + nt_dot(right[1], left[0]))
        return carry

    def finish_row(which, out, s, carry):
        for hop in range(1, reps):
            came = lax.rem(rep + reps - hop, reps)
            pltpu.make_async_remote_copy(
                src_ref=sums.at[which, came, s],
                dst_ref=sums.at[which, came, s],
                send_sem=give_sem.at[which, s, hop - 1],
                recv_sem=take_sem.at[which, s, hop - 1],
                device_id={"rep": came},
                device_id_type=MESH,
            ).wait_recv()
        sums[which, rep, s] = parts[which, s, rep]
        for j in range(quarter):
            turned = sums[which, :, s, j * width : (j + 1) * width, :].reshape(side, side)
            out[s, j] = nt_dot(eye_ref[...], turned).astype(jnp.bfloat16)
        for hop in range(1, reps):
            exchange(which, s, hop).wait_send()
        return carry

    for c in range(chunks):
        lax.fori_loop(c * chunk, (c + 1) * chunk, early_row, 0)
        forward(1, c)
    forward_edge(1)
    lax.fori_loop(0, rows, functools.partial(finish_row, 0, outp_ref), 0)
    settle(1)
    for started in (*sent[0], *sent[1]):
        started.wait_send()
    lax.fori_loop(0, rows, late_row, 0)
    lax.fori_loop(0, rows, functools.partial(finish_row, 1, outd_ref), 0)


def step(margin, reps, table, bits, pick, eye, p_blocks, d_blocks):
    rows, slots, side, _ = p_blocks.shape
    width, quarter = side // reps, slots // reps
    chunks = rows // (margin - 2 * rows)
    shape = jax.ShapeDtypeStruct((rows, quarter, side, side), jnp.bfloat16)
    vmem = pl.BlockSpec(memory_space=pltpu.VMEM)
    smem = pl.BlockSpec(memory_space=pltpu.SMEM)
    return pl.pallas_call(
        functools.partial(step_kernel, margin),
        in_specs=[smem, smem, vmem, vmem, vmem, vmem],
        out_specs=[vmem, vmem],
        out_shape=[shape, shape],
        scratch_shapes=[
            pltpu.VMEM(((rows + 2 * margin) * slots + 1, width, side), jnp.bfloat16),
            pltpu.VMEM(((rows + 2 * margin) * slots + 1, width, side), jnp.bfloat16),
            pltpu.VMEM((3, slots * width, slots * side), jnp.bfloat16),
            pltpu.VMEM((2, side, slots * side), jnp.bfloat16),
            pltpu.VMEM((rows, slots * width, side), jnp.float32),
            pltpu.VMEM((2, rows, reps, quarter * width, side), jnp.bfloat16),
            pltpu.VMEM((2, reps, rows, quarter * width, side), jnp.bfloat16),
            pltpu.SemaphoreType.DMA((2, 4 * chunks + 2)),
            pltpu.SemaphoreType.DMA((2, 4 * chunks + 2)),
            pltpu.SemaphoreType.DMA((2, rows, reps - 1)),
            pltpu.SemaphoreType.DMA((2, rows, reps - 1)),
        ],
        compiler_params=pltpu.CompilerParams(
            collective_id=0, has_side_effects=True, vmem_limit_bytes=48 * 1024 * 1024
        ),
    )(table, bits, pick, eye, p_blocks, d_blocks)


def local(p_blocks, d_blocks, p_cols, d_cols, out_pcols, out_dcols, row_slot, branch):
    rows, slots, side = p_blocks.shape[:3]
    reps, count = lax.axis_size("rep"), lax.axis_size("rows")
    width = side // reps
    all_rows = rows * count
    margin = slots + 2 * MOVE
    row_start = lax.axis_index("rows") * rows
    rep = lax.axis_index("rep")

    pick = (
        jnp.arange(width, dtype=jnp.int32)[:, None] + rep * width
        == jnp.arange(side, dtype=jnp.int32)[None, :]
    ).astype(jnp.bfloat16)
    eye = jnp.eye(side, dtype=jnp.bfloat16)
    nothing = (rows + 2 * margin) * slots

    own_p = lax.dynamic_slice_in_dim(p_cols, row_start, rows, 0)
    own_d = lax.dynamic_slice_in_dim(d_cols, row_start, rows, 0)
    every = jnp.arange(all_rows, dtype=jnp.int32)
    slot_range = jnp.arange(slots, dtype=jnp.int32)
    ids = jnp.concatenate([own_p, own_d]).reshape(-1)
    stored = jnp.sum(jnp.where(ids[:, None] == every, row_slot, 0), axis=1)
    near = ((stored - row_start + margin) % all_rows).reshape(2, rows, slots)
    one_hot = (stored[:, None] == every).astype(jnp.float32)
    columns = jnp.concatenate([p_cols, d_cols], axis=1).astype(jnp.float32)
    named = jnp.dot(one_hot, columns, precision=lax.Precision.HIGHEST)
    named = jnp.round(named).astype(jnp.int32).reshape(2, rows, slots, 2, slots)

    def entries(left, which, out_ids):
        matches = named[left, :, :, which, :, None] == out_ids[:, None, None, :]
        m = jnp.sum(jnp.where(matches, slot_range[:, None] + 1, 0), axis=2)
        return jnp.where(m > 0, near[left, :, :, None] * slots + m - 1, nothing)

    def positions(ids, out_ids):
        matches = ids[:, :, None] == out_ids[:, None, :]
        found = jnp.sum(jnp.where(matches, slot_range[:, None] + 1, 0), axis=1)
        own = margin + jnp.arange(rows, dtype=jnp.int32)[:, None]
        return jnp.where(found > 0, own * slots + found - 1, nothing)

    table = jnp.concatenate(
        [
            entries(0, 0, out_pcols).reshape(-1),
            entries(0, 1, out_dcols).reshape(-1),
            entries(1, 0, out_dcols).reshape(-1),
            positions(own_p, out_pcols).reshape(-1),
            positions(own_d, out_dcols).reshape(-1),
        ]
    ).astype(jnp.int32)
    next_p, next_d = step(margin, reps, table, branch, pick, eye, p_blocks, d_blocks)
    return next_p, next_d


def solution(mesh):
    return jax.shard_map(
        local,
        mesh=mesh,
        in_specs=(
            P("rows", None, None, None),
            P("rows", None, None, None),
            P(),
            P(),
            P("rows", None),
            P("rows", None),
            P(),
            P("rows"),
        ),
        out_specs=(P("rows", "rep", None, None), P("rows", "rep", None, None)),
        check_vma=False,
    )
```
